32 devices in a mesh: ka: 4 (over x, core), ga: 8 (over z, y).
Axes of the slice: x: 2, y: 2, z: 4, core: 2. Of those that a mesh axis runs over, the one named last changes fastest.
Arguments:
- pair_vc: bfloat16 [384, 2048, 128], P('ka', 'ga'), may hold values from -6 to 6
- coulomb: float32 [2048], P('ga'), may hold values from 0.01 to 0.1
- dens_cc: bfloat16 [2, 384, 2048, 128], P(None, 'ka', 'ga'), may hold values from -1.5 to 1.5
- dens_vv: bfloat16 [2, 384, 2048, 128], P(None, 'ka', 'ga'), may hold values from -1.5 to 1.5
- screen: bfloat16 [2, 2048, 2048], P(None, 'ga'), may hold values from -0.125 to 0.125
- offsets: int32 [2, 2], replicated, may hold values from 0 to 23, as said below
Outputs:
- kernel: float32 [2, 2, 384, 4096], P(None, None, ('ka', 'ga'))
The draws below stay inside these ranges and needn't reach their ends.
Inputs may be any that keep to these rules, and one draw needn't show every extreme that they name: offsets[o, 0] is 1 to 4; one offset, which one drawn from the seed, has offsets[o, 0] = 4 and offsets[o, 1] = 23, the other has offsets[o, 1] = 0.
All inputs are finite; a program needn't handle non-finite values.
Results may differ from the reference program's by a relative error of at most 0.0029.
Values may be sent and summed in bfloat16 or wider, within the bound.
A program may use at most 192 MiB of HBM per device.

```python
import math
import jax
import jax.numpy as jnp
from jax import lax

NV = 8
NC = 8
NG = 2048
NKY = 24
KX_DEV = 4
NOFF = 2
NKX = 16
NK = 384


def draw_offsets(key, part):
    key = jax.random.fold_in(key, 11)
    first_key, second_key = jax.random.split(key, 2)
    special = jax.random.randint(first_key, (), 0, NOFF)
    row_index = jnp.arange(NOFF)
    steps_x = jax.random.randint(second_key, (NOFF,), 1, KX_DEV + 1)
    steps_x = jnp.where(row_index == special, KX_DEV, steps_x)
    steps_y = jnp.where(row_index == special, NKY - 1, 0)
    return jnp.stack([steps_x, steps_y], axis=1).astype(jnp.int32)


def block_levels(own_key, extent, pieces, low, top_value):
    def one(dim, shards_of):
        heights = jax.random.uniform(jax.random.fold_in(jax.random.fold_in(own_key, 6), dim), (shards_of,), jnp.float32, low / len(pieces), top_value / len(pieces))
        return jnp.repeat(jnp.exp(heights), extent[dim] // shards_of).reshape((-1,) + (1,) * (len(extent) - dim - 1))

    gain = one(*pieces[0])
    for cut in pieces[1:]:
        gain = gain * one(*cut)
    return gain


def bell_draw(own_key, shape, deviation, reach, pieces=(), dtype=jnp.bfloat16):
    array = jax.random.normal(own_key, shape, jnp.float32) * deviation
    if len(pieces) > 0:
        array = block_levels(own_key, shape, pieces, -0.22, 0.18) * array
    return jnp.clip(array, min=-reach, max=reach).astype(dtype)


def setup_inputs(seed: int = 0) -> dict:
    key_of = jax.random.split(jax.random.key(seed), 7)
    pair_vc = bell_draw(key_of[0], (NK, NG, 2 * NV * NC), 1.0, 6.0, ((0, 4), (1, 8)))
    coulomb = jnp.clip(jnp.exp(math.log(0.1) - 2.3025851 * jax.random.uniform(key_of[1], (NG,), jnp.float32) ** block_levels(key_of[1], (NG,), ((0, 8),), -0.2, 0.2)), 0.01, 0.1)
    dens_cc = bell_draw(key_of[2], (NOFF, NK, NG, 2 * NC * NC), 0.25, 1.5, ((1, 4), (2, 8)))
    dens_vv = bell_draw(key_of[3], (NOFF, NK, NG, 2 * NV * NV), 0.25, 1.5, ((1, 4), (2, 8)))
    screen = bell_draw(key_of[4], (NOFF, NG, NG), NG ** -0.5, 0.125, ((1, 8),))
    offsets = draw_offsets(jax.random.fold_in(key_of[6], 71), 0)
    return {"pair_vc": pair_vc, "coulomb": coulomb, "dens_cc": dens_cc, "dens_vv": dens_vv, "screen": screen, "offsets": offsets}


def to_planes(field, width):
    shaped = field.astype(jnp.float32).reshape(NK, NG, 2, width)
    return jnp.transpose(shaped, (2, 0, 3, 1))


def shift_grid(field, step_x, step_y):
    twice = jnp.concatenate([field, field], axis=1)
    field = lax.dynamic_slice_in_dim(twice, step_x, NKX, 1)
    twice = jnp.concatenate([field, field], axis=2)
    return lax.dynamic_slice_in_dim(twice, step_y, NKY, 2)


def pair_products(left_side, right_side):
    real_real = jnp.einsum('kpg,kqg->kpq', left_side[0], right_side[0])
    imag_imag = jnp.einsum('kpg,kqg->kpq', left_side[1], right_side[1])
    real_imag = jnp.einsum('kpg,kqg->kpq', left_side[0], right_side[1])
    imag_real = jnp.einsum('kpg,kqg->kpq', left_side[1], right_side[0])
    return jnp.stack([real_real + imag_imag, real_imag - imag_real])


def reorder_direct(direct):
    shaped = direct.reshape(2, NK, NC, NC, NV, NV)
    shaped = jnp.transpose(shaped, (0, 1, 4, 2, 5, 3))
    return shaped.reshape(2, NK, NV * NC * NV * NC)


def reference(pair_vc, coulomb, dens_cc, dens_vv, screen, offsets):
    pairs = NV * NC
    widened = to_planes(pair_vc, pairs)
    scaled = lax.optimization_barrier((coulomb * widened).astype(jnp.bfloat16)).astype(jnp.float32)
    grid = widened.reshape(2, NKX, NKY, pairs, NG)
    kernels = []
    for offset_index in range(NOFF):
        step_x = offsets[offset_index, 0].astype(jnp.int32)
        step_y = offsets[offset_index, 1].astype(jnp.int32)
        moved = shift_grid(grid, step_x, step_y).reshape(2, NK, pairs, NG)
        exch = pair_products(scaled, moved).reshape(2, NK, pairs * pairs)
        valence = to_planes(dens_vv[offset_index], NV * NV)
        conduction = to_planes(dens_cc[offset_index], NC * NC)
        image = jnp.einsum('gh,ckph->ckpg', screen[offset_index].astype(jnp.float32), valence)
        image = lax.optimization_barrier(image.astype(jnp.bfloat16)).astype(jnp.float32)
        direct = pair_products(conduction, image)
        kernels.append(2.0 * exch - reorder_direct(direct))
    return jnp.stack(kernels)
```

```python
import functools

import jax
import jax.numpy as jnp
from jax import lax
from jax.experimental import pallas as pl
from jax.experimental.pallas import tpu as pltpu
from jax.sharding import PartitionSpec as P

NV = 8
NC = 8
NKY = 24
NOFF = 2
WINDOW = 10
MESH = pl.DeviceIdType.MESH


def step_order(length):
    order = []
    for i in range(length):
        step = length // 2 + (i + 1) // 2 * (1 if i % 2 else -1)
        if 0 < step < length:
            order.append(step)
    return order


def over_rows(left, right):
    return lax.dot_general(
        left, right, (((0,), (0,)), ((), ())), preferred_element_type=jnp.float32
    )


def block_transpose(tile):
    row = lax.broadcasted_iota(jnp.int32, tile.shape, 1)
    lane = lax.broadcasted_iota(jnp.int32, tile.shape, 2)
    for bit in range(3):
        size = 1 << bit
        row_bit = (row // size) % 2
        lane_bit = (lane // (8 * size)) % 2
        down = pltpu.roll(pltpu.roll(tile, 8 - size, 1), 8 * size, 2)
        up = pltpu.roll(pltpu.roll(tile, size, 1), 128 - 8 * size, 2)
        tile = jnp.where(row_bit == lane_bit, tile, jnp.where(row_bit == 0, down, up))
    return tile


def kernel(
    shards, groups, offsets, coulomb, pair_vc, dens_cc, dens_vv, screen,
    out, cc_land, vv_land,
    both, ex_send, ex_recv, wide, vv_here, cc_here, image, rows,
    send_sem, recv_sem, ka_send, ka_recv, own_sem, load_sem,
):
    me = lax.axis_index("ga")
    my_ka = lax.axis_index("ka")
    local_k, slab, _ = pair_vc.shape
    few_k = local_k // shards
    quarter = slab // groups
    steps = step_order(shards)
    lane = lax.broadcasted_iota(jnp.int32, (64, 128), 1)
    sign = jnp.where(lane < 64, 1.0, -1.0)

    barrier = pltpu.get_barrier_semaphore()
    for step in range(1, shards):
        pl.semaphore_signal(
            barrier, inc=1, device_id={"ga": (me + step) % shards}, device_id_type=MESH
        )
    for step in range(1, groups):
        pl.semaphore_signal(
            barrier, inc=1, device_id={"ka": (my_ka + step) % groups}, device_id_type=MESH
        )
    pl.semaphore_wait(barrier, shards - 1 + groups - 1)

    def own(index, source, target):
        return pltpu.make_async_copy(source, target, own_sem.at[index])

    def to_ga(kind, step, source, target):
        return pltpu.make_async_remote_copy(
            src_ref=source,
            dst_ref=target,
            send_sem=send_sem.at[kind, step],
            recv_sem=recv_sem.at[kind, step],
            device_id={"ga": (me + step) % shards},
            device_id_type=MESH,
        )

    def to_ka(index, step, source, target):
        return pltpu.make_async_remote_copy(
            src_ref=source,
            dst_ref=target,
            send_sem=ka_send.at[index],
            recv_sem=ka_recv.at[index],
            device_id={"ka": (my_ka + step) % groups},
            device_id_type=MESH,
        )

    def dens_copies(kind, dens, land, offset):
        return [
            to_ga(
                kind,
                step,
                dens.at[offset, pl.ds(((me + step) % shards) * few_k, few_k)],
                land.at[offset, :, me],
            )
            for step in steps
        ]

    ahead = to_ka(0, groups - 1, pair_vc, both.at[pl.ds(local_k, local_k)])
    ahead.start()
    my_rows = screen.at[:, pl.ds(my_ka * quarter, quarter)]
    screen_ga = [to_ga(4, step, my_rows, wide.at[:, me, my_ka]) for step in steps]
    for copy in screen_ga:
        copy.start()
    mine = [
        own(0, pair_vc, both.at[pl.ds(0, local_k)]),
        own(1, my_rows, wide.at[:, me, my_ka]),
    ]
    for offset in range(NOFF):
        for index, dens, land in ((2, dens_cc, cc_land), (3, dens_vv, vv_land)):
            mine.append(
                own(
                    index + 2 * offset,
                    dens.at[offset, pl.ds(me * few_k, few_k)],
                    land.at[offset, :, me],
                )
            )
    for copy in mine:
        copy.start()

    vv_copies = [dens_copies(offset, dens_vv, vv_land, offset) for offset in range(NOFF)]
    cc_copies = [dens_copies(2 + offset, dens_cc, cc_land, offset) for offset in range(NOFF)]
    queue = []
    for offset in range(NOFF):
        queue += vv_copies[offset] + cc_copies[offset]
    sent = [0, 0]

    def finish(count):
        for _ in range(count):
            queue[sent[1]].wait_send()
            sent[1] += 1
            if sent[0] < len(queue):
                queue[sent[0]].start()
                sent[0] += 1

    while sent[0] < min(WINDOW, len(queue)):
        queue[sent[0]].start()
        sent[0] += 1

    for copy in screen_ga:
        copy.wait_recv()
    mine[1].wait()
    screen_ka = [
        to_ka(step, step, wide.at[:, :, my_ka], wide.at[:, :, my_ka])
        for step in range(1, groups)
    ]
    for copy in screen_ka:
        copy.start()

    mine[0].wait()
    ahead.wait_recv()

    def one_exchange(k, carry):
        scaled = (coulomb[...] * both[k].astype(jnp.float32)).astype(jnp.bfloat16)
        row, column = k // NKY, k % NKY
        for offset in range(NOFF):
            moved_column = column + offsets[offset, 1]
            moved_column = jnp.where(moved_column >= NKY, moved_column - NKY, moved_column)
            partner = (row + offsets[offset, 0]) * NKY + moved_column
            full = over_rows(scaled, both[partner])
            summed = full[:64] + sign * pltpu.roll(full[64:], 64, 1)
            ex_send[offset, k] = summed.astype(jnp.bfloat16)
        return carry

    lax.fori_loop(0, local_k, one_exchange, 0)
    ex_copies = [
        to_ga(
            5,
            step,
            ex_send.at[:, pl.ds(((me + step) % shards) * few_k, few_k)],
            ex_recv.at[step],
        )
        for step in steps
    ]
    for copy in ex_copies:
        copy.start()

    together = 2 if few_k % 2 == 0 else 1
    big = slab * shards

    for offset in range(NOFF):
        finish(len(steps))
        for copy in vv_copies[offset]:
            copy.wait_recv()
        mine[3 + 2 * offset].wait()
        load = pltpu.make_async_copy(vv_land.at[offset], vv_here, load_sem.at[0])
        load.start()
        if offset == 0:
            for copy in screen_ka:
                copy.wait_recv()
        load.wait()

        def one_image(index, carry, offset=offset):
            first = (index // shards) * together
            part = index % shards
            right = jnp.concatenate(
                [vv_here[first + i].reshape(big, 128) for i in range(together)], axis=1
            )
            left = wide[offset, part].reshape(slab, big)
            made = jnp.dot(left, right, preferred_element_type=jnp.float32)
            made = made.astype(jnp.bfloat16)
            for i in range(together):
                image[first + i, part] = made[:, i * 128 : (i + 1) * 128]
            return carry

        lax.fori_loop(0, few_k // together * shards, one_image, 0)

        finish(len(steps))
        if offset == 0:
            for copy in ex_copies:
                copy.wait_recv()
        for copy in cc_copies[offset]:
            copy.wait_recv()
        mine[2 + 2 * offset].wait()
        load = pltpu.make_async_copy(cc_land.at[offset], cc_here, load_sem.at[1])
        load.start()
        load.wait()

        def one_direct(k, carry, offset=offset):
            full = over_rows(image[k].reshape(big, 128), cc_here[k].reshape(big, 128))
            summed = pltpu.roll(full[64:], 64, 1) + sign * full[:64]
            direct = block_transpose(summed.reshape(8, 8, 128)).reshape(64, 128)
            exchange = ex_send[offset, me * few_k + k].astype(jnp.float32)
            for step in range(1, shards):
                exchange = exchange + ex_recv[step, offset, k].astype(jnp.float32)
            rows[k] = 2.0 * exchange - direct
            return carry

        lax.fori_loop(0, few_k, one_direct, 0)
        narrow = lax.broadcasted_iota(jnp.int32, (few_k, 128), 1) < 64
        for pair in range(32):
            even, odd = rows[:, 2 * pair, :], rows[:, 2 * pair + 1, :]
            place = pl.ds(pair * 128, 128)
            out[offset, 0, :, place] = jnp.where(narrow, even, pltpu.roll(odd, 64, 1))
            out[offset, 1, :, place] = jnp.where(narrow, pltpu.roll(even, 64, 1), odd)

    ahead.wait_send()
    for copy in screen_ga + screen_ka + ex_copies:
        copy.wait_send()


def local(shards, groups, pair_vc, coulomb, dens_cc, dens_vv, screen, offsets):
    local_k, slab, width = pair_vc.shape
    few_k = local_k // shards
    big = slab * shards
    spread = jnp.broadcast_to(coulomb[:, None], (slab, width))
    land = jax.ShapeDtypeStruct((NOFF, few_k, shards, slab, width), jnp.bfloat16)
    anywhere = pl.BlockSpec(memory_space=pl.ANY)
    in_vmem = pl.BlockSpec(memory_space=pltpu.VMEM)
    flops = 2 * NOFF * (few_k * big * big * width + 2 * few_k * big * width * width)
    result = pl.pallas_call(
        functools.partial(kernel, shards, groups),
        out_shape=[
            jax.ShapeDtypeStruct((NOFF, 2, few_k, 4096), jnp.float32),
            land,
            land,
        ],
        in_specs=[pl.BlockSpec(memory_space=pltpu.SMEM), in_vmem] + [anywhere] * 4,
        out_specs=[in_vmem, anywhere, anywhere],
        scratch_shapes=[
            pltpu.VMEM((2 * local_k, slab, width), jnp.bfloat16),
            pltpu.VMEM((NOFF, local_k, 64, 128), jnp.bfloat16),
            pltpu.VMEM((shards, NOFF, few_k, 64, 128), jnp.bfloat16),
            pltpu.VMEM((NOFF, shards, groups, slab // groups, big), jnp.bfloat16),
            pltpu.VMEM((few_k, shards, slab, width), jnp.bfloat16),
            pltpu.VMEM((few_k, shards, slab, width), jnp.bfloat16),
            pltpu.VMEM((few_k, shards, slab, width), jnp.bfloat16),
            pltpu.VMEM((few_k, 64, 128), jnp.float32),
            pltpu.SemaphoreType.DMA((6, shards)),
            pltpu.SemaphoreType.DMA((6, shards)),
            pltpu.SemaphoreType.DMA((groups,)),
            pltpu.SemaphoreType.DMA((groups,)),
            pltpu.SemaphoreType.DMA((6,)),
            pltpu.SemaphoreType.DMA((2,)),
        ],
        compiler_params=pltpu.CompilerParams(
            collective_id=0, has_side_effects=True, vmem_limit_bytes=60 * 1024 * 1024
        ),
        cost_estimate=pl.CostEstimate(flops=flops, bytes_accessed=80_000_000, transcendentals=0),
        name="bse_blocks",
    )(offsets, spread, pair_vc, dens_cc, dens_vv, screen)
    return result[0]


def solution(mesh):
    placed = (
        P("ka", "ga", None),
        P("ga"),
        P(None, "ka", "ga", None),
        P(None, "ka", "ga", None),
        P(None, "ga", None),
        P(),
    )
    return jax.shard_map(
        functools.partial(local, mesh.shape["ga"], mesh.shape["ka"]),
        mesh=mesh,
        in_specs=placed,
        out_specs=P(None, None, ("ka", "ga"), None),
        check_vma=False,
    )
```

```python
import functools

import jax
import jax.numpy as jnp
from jax import lax
from jax.experimental import pallas as pl
from jax.experimental.pallas import tpu as pltpu
from jax.sharding import PartitionSpec as P

NV = 8
NC = 8
NKY = 24
NOFF = 2
WINDOW = 10
MESH = pl.DeviceIdType.MESH


def step_order(length):
    order = []
    for i in range(length):
        step = length // 2 + (i + 1) // 2 * (1 if i % 2 else -1)
        if 0 < step < length:
            order.append(step)
    return order


def over_rows(left, right):
    return lax.dot_general(
        left, right, (((0,), (0,)), ((), ())), preferred_element_type=jnp.float32
    )


def block_transpose(tile):
    row = lax.broadcasted_iota(jnp.int32, tile.shape, 1)
    lane = lax.broadcasted_iota(jnp.int32, tile.shape, 2)
    for bit in range(3):
        size = 1 << bit
        row_bit = (row // size) % 2
        lane_bit = (lane // (8 * size)) % 2
        down = pltpu.roll(pltpu.roll(tile, 8 - size, 1), 8 * size, 2)
        up = pltpu.roll(pltpu.roll(tile, size, 1), 128 - 8 * size, 2)
        tile = jnp.where(row_bit == lane_bit, tile, jnp.where(row_bit == 0, down, up))
    return tile


def kernel(
    shards, groups, offsets, coulomb, pair_vc, dens_cc, dens_vv, screen,
    out, cc_land, vv_land,
    both, ex, ex_recv, far_send, far_recv, wide, vv_here, cc_here, image, rows,
    send_sem, recv_sem, ka_send, ka_recv, own_sem, load_sem,
):
    me = lax.axis_index("ga")
    my_ka = lax.axis_index("ka")
    local_k, slab, _ = pair_vc.shape
    few_k = local_k // shards
    quarter = slab // groups
    steps = step_order(shards)
    lane = lax.broadcasted_iota(jnp.int32, (64, 128), 1)
    sign = jnp.where(lane < 64, 1.0, -1.0)

    barrier = pltpu.get_barrier_semaphore()
    for step in range(1, shards):
        pl.semaphore_signal(
            barrier, inc=1, device_id={"ga": (me + step) % shards}, device_id_type=MESH
        )
    for step in range(1, groups):
        pl.semaphore_signal(
            barrier, inc=1, device_id={"ka": (my_ka + step) % groups}, device_id_type=MESH
        )
    pl.semaphore_wait(barrier, shards - 1 + groups - 1)

    def own(index, source, target):
        return pltpu.make_async_copy(source, target, own_sem.at[index])

    def to_ga(kind, step, source, target):
        return pltpu.make_async_remote_copy(
            src_ref=source,
            dst_ref=target,
            send_sem=send_sem.at[kind, step],
            recv_sem=recv_sem.at[kind, step],
            device_id={"ga": (me + step) % shards},
            device_id_type=MESH,
        )

    def partner_of(distance):
        return me + distance - 2 * distance * ((me // distance) % 2)

    def to_partner(kind, index, distance, source, target):
        return pltpu.make_async_remote_copy(
            src_ref=source,
            dst_ref=target,
            send_sem=send_sem.at[kind, index],
            recv_sem=recv_sem.at[kind, index],
            device_id={"ga": partner_of(distance)},
            device_id_type=MESH,
        )

    def to_ka(index, step, source, target):
        return pltpu.make_async_remote_copy(
            src_ref=source,
            dst_ref=target,
            send_sem=ka_send.at[index],
            recv_sem=ka_recv.at[index],
            device_id={"ka": (my_ka + step) % groups},
            device_id_type=MESH,
        )

    def dens_copies(kind, dens, land, offset):
        return [
            to_ga(
                kind,
                step,
                dens.at[offset, pl.ds(((me + step) % shards) * few_k, few_k)],
                land.at[offset, :, me],
            )
            for step in steps
        ]

    ahead = to_ka(0, groups - 1, pair_vc, both.at[pl.ds(local_k, local_k)])
    ahead.start()
    my_rows = screen.at[:, pl.ds(my_ka * quarter, quarter)]
    screen_hops = []
    distance = shards // 2
    taken = 0
    while distance >= 1:
        hop = []
        for i in range(shards // (2 * distance)):
            block = me % (2 * distance) + 2 * distance * i
            place = wide.at[:, block, my_ka]
            hop.append(to_partner(4, taken, distance, my_rows if taken == 0 else place, place))
            taken += 1
        screen_hops.append(hop)
        distance //= 2
    screen_ga = sum(screen_hops, [])
    for copy in screen_hops[0]:
        copy.start()
    mine = [
        own(0, pair_vc, both.at[pl.ds(0, local_k)]),
        own(1, my_rows, wide.at[:, me, my_ka]),
    ]
    for offset in range(NOFF):
        for index, dens, land in ((2, dens_cc, cc_land), (3, dens_vv, vv_land)):
            mine.append(
                own(
                    index + 2 * offset,
                    dens.at[offset, pl.ds(me * few_k, few_k)],
                    land.at[offset, :, me],
                )
            )
    for copy in mine:
        copy.start()

    vv_copies = [dens_copies(offset, dens_vv, vv_land, offset) for offset in range(NOFF)]
    cc_copies = [dens_copies(2 + offset, dens_cc, cc_land, offset) for offset in range(NOFF)]
    queue = []
    for offset in range(NOFF):
        queue += vv_copies[offset] + cc_copies[offset]
    sent = [0, 0]

    def finish(count):
        for _ in range(count):
            queue[sent[1]].wait_send()
            sent[1] += 1
            if sent[0] < len(queue):
                queue[sent[0]].start()
                sent[0] += 1

    while sent[0] < min(WINDOW, len(queue)):
        queue[sent[0]].start()
        sent[0] += 1

    mine[1].wait()
    for index, hop in enumerate(screen_hops):
        for copy in hop:
            copy.wait_recv()
        if index + 1 < len(screen_hops):
            for copy in screen_hops[index + 1]:
                copy.start()
    screen_ka = [
        to_ka(step, step, wide.at[:, :, my_ka], wide.at[:, :, my_ka])
        for step in range(1, groups)
    ]
    for copy in screen_ka:
        copy.start()

    mine[0].wait()
    ahead.wait_recv()

    def one_exchange(k, carry):
        scaled = (coulomb[...] * both[k].astype(jnp.float32)).astype(jnp.bfloat16)
        row, column = k // NKY, k % NKY
        for offset in range(NOFF):
            moved_column = column + offsets[offset, 1]
            moved_column = jnp.where(moved_column >= NKY, moved_column - NKY, moved_column)
            partner = (row + offsets[offset, 0]) * NKY + moved_column
            full = over_rows(scaled, both[partner])
            summed = full[:64] + sign * pltpu.roll(full[64:], 64, 1)
            ex[offset, k // few_k, k % few_k] = summed
        return carry

    lax.fori_loop(0, local_k, one_exchange, 0)
    hops = []
    distance = 1
    taken = 0
    while distance < shards:
        hop = []
        for i in range(shards // (2 * distance)):
            block = partner_of(distance) % (2 * distance) + 2 * distance * i
            if 2 * distance < shards:
                source, target = ex.at[:, block], ex_recv.at[taken]
            else:
                source, target = far_send, far_recv
            hop.append((to_partner(5, taken, distance, source, target), taken, distance, i))
            taken += 1
        hops.append(hop)
        distance *= 2
    ex_copies = [copy for hop in hops for copy, _, _, _ in hop]

    def start_hop(index):
        if index + 1 == len(hops):
            far_send[...] = ex[:, partner_of(shards // 2)].astype(jnp.bfloat16)
        for copy, _, _, _ in hops[index]:
            copy.start()

    def end_hop(index):
        for copy, slot, distance, i in hops[index]:
            copy.wait()
            if index + 1 < len(hops):
                block = me % (2 * distance) + 2 * distance * i

                def add(k, carry, slot=slot, block=block):
                    for offset in range(NOFF):
                        ex[offset, block, k] = ex[offset, block, k] + ex_recv[slot, offset, k]
                    return carry

                lax.fori_loop(0, few_k, add, 0)

    start_hop(0)

    rows[...] = jnp.zeros_like(rows)

    def write_out(offset):
        narrow = lax.broadcasted_iota(jnp.int32, (few_k, 128), 1) < 64
        for pair in range(32):
            even, odd = rows[offset, :, 2 * pair, :], rows[offset, :, 2 * pair + 1, :]
            place = pl.ds(pair * 128, 128)
            out[offset, 0, :, place] = jnp.where(narrow, even, pltpu.roll(odd, 64, 1))
            out[offset, 1, :, place] = jnp.where(narrow, pltpu.roll(even, 64, 1), odd)

    together = 2 if few_k % 2 == 0 else 1
    big = slab * shards

    for offset in range(NOFF):
        finish(len(steps))
        for copy in vv_copies[offset]:
            copy.wait_recv()
        mine[3 + 2 * offset].wait()
        load = pltpu.make_async_copy(vv_land.at[offset], vv_here, load_sem.at[0])
        load.start()
        if offset == 0:
            for copy in screen_ka:
                copy.wait_recv()
        load.wait()

        def one_image(index, carry, offset=offset):
            first = (index // shards) * together
            part = index % shards
            right = jnp.concatenate(
                [vv_here[first + i].reshape(big, 128) for i in range(together)], axis=1
            )
            left = wide[offset, part].reshape(slab, big)
            made = jnp.dot(left, right, preferred_element_type=jnp.float32)
            made = made.astype(jnp.bfloat16)
            for i in range(together):
                image[first + i, part] = made[:, i * 128 : (i + 1) * 128]
            return carry

        lax.fori_loop(0, few_k // together * shards, one_image, 0)
        if offset == 0:
            end_hop(0)
            start_hop(1)
        else:
            end_hop(len(hops) - 1)

            def add_far(k, carry):
                for each in range(NOFF):
                    total = ex[each, me, k] + far_recv[each, k].astype(jnp.float32)
                    rows[each, k] = rows[each, k] + 2.0 * total
                return carry

            lax.fori_loop(0, few_k, add_far, 0)
            write_out(0)

        finish(len(steps))
        for copy in cc_copies[offset]:
            copy.wait_recv()
        mine[2 + 2 * offset].wait()
        load = pltpu.make_async_copy(cc_land.at[offset], cc_here, load_sem.at[1])
        load.start()
        load.wait()

        def one_direct(k, carry, offset=offset):
            full = over_rows(image[k].reshape(big, 128), cc_here[k].reshape(big, 128))
            summed = pltpu.roll(full[64:], 64, 1) + sign * full[:64]
            direct = block_transpose(summed.reshape(8, 8, 128)).reshape(64, 128)
            rows[offset, k] = rows[offset, k] - direct
            return carry

        lax.fori_loop(0, few_k, one_direct, 0)
        if offset == 0:
            for index in range(1, len(hops) - 1):
                end_hop(index)
                start_hop(index + 1)
    write_out(1)

    ahead.wait_send()
    for copy in screen_ga + screen_ka:
        copy.wait_send()


def local(shards, groups, pair_vc, coulomb, dens_cc, dens_vv, screen, offsets):
    local_k, slab, width = pair_vc.shape
    few_k = local_k // shards
    big = slab * shards
    spread = jnp.broadcast_to(coulomb[:, None], (slab, width))
    land = jax.ShapeDtypeStruct((NOFF, few_k, shards, slab, width), jnp.bfloat16)
    anywhere = pl.BlockSpec(memory_space=pl.ANY)
    in_vmem = pl.BlockSpec(memory_space=pltpu.VMEM)
    flops = 2 * NOFF * (few_k * big * big * width + 2 * few_k * big * width * width)
    result = pl.pallas_call(
        functools.partial(kernel, shards, groups),
        out_shape=[
            jax.ShapeDtypeStruct((NOFF, 2, few_k, 4096), jnp.float32),
            land,
            land,
        ],
        in_specs=[pl.BlockSpec(memory_space=pltpu.SMEM), in_vmem] + [anywhere] * 4,
        out_specs=[in_vmem, anywhere, anywhere],
        scratch_shapes=[
            pltpu.VMEM((2 * local_k, slab, width), jnp.bfloat16),
            pltpu.VMEM((NOFF, shards, few_k, 64, 128), jnp.float32),
            pltpu.VMEM((shards - 2, NOFF, few_k, 64, 128), jnp.float32),
            pltpu.VMEM((NOFF, few_k, 64, 128), jnp.bfloat16),
            pltpu.VMEM((NOFF, few_k, 64, 128), jnp.bfloat16),
            pltpu.VMEM((NOFF, shards, groups, slab // groups, big), jnp.bfloat16),
            pltpu.VMEM((few_k, shards, slab, width), jnp.bfloat16),
            pltpu.VMEM((few_k, shards, slab, width), jnp.bfloat16),
            pltpu.VMEM((few_k, shards, slab, width), jnp.bfloat16),
            pltpu.VMEM((NOFF, few_k, 64, 128), jnp.float32),
            pltpu.SemaphoreType.DMA((6, shards)),
            pltpu.SemaphoreType.DMA((6, shards)),
            pltpu.SemaphoreType.DMA((groups,)),
            pltpu.SemaphoreType.DMA((groups,)),
            pltpu.SemaphoreType.DMA((6,)),
            pltpu.SemaphoreType.DMA((2,)),
        ],
        compiler_params=pltpu.CompilerParams(
            collective_id=0, has_side_effects=True, vmem_limit_bytes=62 * 1024 * 1024
        ),
        cost_estimate=pl.CostEstimate(flops=flops, bytes_accessed=80_000_000, transcendentals=0),
        name="bse_blocks",
    )(offsets, spread, pair_vc, dens_cc, dens_vv, screen)
    return result[0]


def solution(mesh):
    placed = (
        P("ka", "ga", None),
        P("ga"),
        P(None, "ka", "ga", None),
        P(None, "ka", "ga", None),
        P(None, "ga", None),
        P(),
    )
    return jax.shard_map(
        functools.partial(local, mesh.shape["ga"], mesh.shape["ka"]),
        mesh=mesh,
        in_specs=placed,
        out_specs=P(None, None, ("ka", "ga"), None),
        check_vma=False,
    )
```

```python
import functools

import jax
import jax.numpy as jnp
from jax import lax
from jax.experimental import pallas as pl
from jax.experimental.pallas import tpu as pltpu
from jax.sharding import PartitionSpec as P

NV = 8
NC = 8
NKY = 24
NOFF = 2
MESH = pl.DeviceIdType.MESH


def step_order(length):
    order = []
    for i in range(length):
        step = length // 2 + (i + 1) // 2 * (1 if i % 2 else -1)
        if 0 < step < length:
            order.append(step)
    return order


def over_rows(left, right):
    return lax.dot_general(
        left, right, (((0,), (0,)), ((), ())), preferred_element_type=jnp.float32
    )


def block_transpose(tile):
    row = lax.broadcasted_iota(jnp.int32, tile.shape, 1)
    lane = lax.broadcasted_iota(jnp.int32, tile.shape, 2)
    for bit in range(3):
        size = 1 << bit
        row_bit = (row // size) % 2
        lane_bit = (lane // (8 * size)) % 2
        down = pltpu.roll(pltpu.roll(tile, 8 - size, 1), 8 * size, 2)
        up = pltpu.roll(pltpu.roll(tile, size, 1), 128 - 8 * size, 2)
        tile = jnp.where(row_bit == lane_bit, tile, jnp.where(row_bit == 0, down, up))
    return tile


def kernel(
    shards, groups, offsets, coulomb, pair_vc, dens_cc, dens_vv, screen,
    out, cc_land, vv_land,
    both, ex, ex_recv, far_send, far_recv, wide, vv_here, cc_here, image, totals, rows,
    send_sem, recv_sem, ka_send, ka_recv, own_sem, load_sem,
):
    me = lax.axis_index("ga")
    my_ka = lax.axis_index("ka")
    local_k, slab, _ = pair_vc.shape
    few_k = local_k // shards
    quarter = slab // groups
    steps = step_order(shards)
    lane = lax.broadcasted_iota(jnp.int32, (64, 128), 1)
    sign = jnp.where(lane < 64, 1.0, -1.0)

    barrier = pltpu.get_barrier_semaphore()
    for step in range(1, shards):
        pl.semaphore_signal(
            barrier, inc=1, device_id={"ga": (me + step) % shards}, device_id_type=MESH
        )
    for step in range(1, groups):
        pl.semaphore_signal(
            barrier, inc=1, device_id={"ka": (my_ka + step) % groups}, device_id_type=MESH
        )
    pl.semaphore_wait(barrier, shards - 1 + groups - 1)

    def own(index, source, target):
        return pltpu.make_async_copy(source, target, own_sem.at[index])

    def to_ga(kind, step, source, target):
        return pltpu.make_async_remote_copy(
            src_ref=source,
            dst_ref=target,
            send_sem=send_sem.at[kind, step],
            recv_sem=recv_sem.at[kind, step],
            device_id={"ga": (me + step) % shards},
            device_id_type=MESH,
        )

    def partner_of(distance):
        return me + distance - 2 * distance * ((me // distance) % 2)

    def to_partner(kind, index, distance, source, target):
        return pltpu.make_async_remote_copy(
            src_ref=source,
            dst_ref=target,
            send_sem=send_sem.at[kind, index],
            recv_sem=recv_sem.at[kind, index],
            device_id={"ga": partner_of(distance)},
            device_id_type=MESH,
        )

    def to_ka(index, step, source, target):
        return pltpu.make_async_remote_copy(
            src_ref=source,
            dst_ref=target,
            send_sem=ka_send.at[index],
            recv_sem=ka_recv.at[index],
            device_id={"ka": (my_ka + step) % groups},
            device_id_type=MESH,
        )

    def dens_copies(kind, dens, land, offset):
        return [
            to_ga(
                kind,
                step,
                dens.at[offset, pl.ds(((me + step) % shards) * few_k, few_k)],
                land.at[offset, :, me],
            )
            for step in steps
        ]

    ahead = to_ka(0, groups - 1, pair_vc, both.at[pl.ds(local_k, local_k)])
    ahead.start()
    my_rows = screen.at[:, pl.ds(my_ka * quarter, quarter)]
    screen_hops = []
    distance = shards // 2
    taken = 0
    while distance >= 1:
        hop = []
        for i in range(shards // (2 * distance)):
            block = me % (2 * distance) + 2 * distance * i
            place = wide.at[:, block, my_ka]
            hop.append(to_partner(4, taken, distance, my_rows if taken == 0 else place, place))
            taken += 1
        screen_hops.append(hop)
        distance //= 2
    screen_ga = sum(screen_hops, [])
    for copy in screen_hops[0]:
        copy.start()
    mine = [
        own(0, pair_vc, both.at[pl.ds(0, local_k)]),
        own(1, my_rows, wide.at[:, me, my_ka]),
    ]
    for offset in range(NOFF):
        for index, dens, land in ((2, dens_cc, cc_land), (3, dens_vv, vv_land)):
            mine.append(
                own(
                    index + 2 * offset,
                    dens.at[offset, pl.ds(me * few_k, few_k)],
                    land.at[offset, :, me],
                )
            )
    for copy in mine:
        copy.start()

    vv_copies = [dens_copies(offset, dens_vv, vv_land, offset) for offset in range(NOFF)]
    cc_copies = [dens_copies(2 + offset, dens_cc, cc_land, offset) for offset in range(NOFF)]
    queue = []
    for offset in range(NOFF):
        queue += vv_copies[offset] + cc_copies[offset]
    sent = [0, 0]

    def finish(count):
        for _ in range(count):
            queue[sent[1]].wait_send()
            sent[1] += 1
            if sent[0] < len(queue):
                queue[sent[0]].start()
                sent[0] += 1

    while sent[0] < 2 * len(steps):
        queue[sent[0]].start()
        sent[0] += 1

    mine[1].wait()
    for index, hop in enumerate(screen_hops):
        for copy in hop:
            copy.wait_recv()
        if index + 1 < len(screen_hops):
            for copy in screen_hops[index + 1]:
                copy.start()
    screen_ka = [
        to_ka(step, step, wide.at[:, :, my_ka], wide.at[:, :, my_ka])
        for step in range(1, groups)
    ]
    for copy in screen_ka:
        copy.start()

    mine[0].wait()
    ahead.wait_recv()

    def one_exchange(k, carry):
        scaled = (coulomb[...] * both[k].astype(jnp.float32)).astype(jnp.bfloat16)
        row, column = k // NKY, k % NKY
        for offset in range(NOFF):
            moved_column = column + offsets[offset, 1]
            moved_column = jnp.where(moved_column >= NKY, moved_column - NKY, moved_column)
            partner = (row + offsets[offset, 0]) * NKY + moved_column
            full = over_rows(scaled, both[partner])
            summed = full[:64] + sign * pltpu.roll(full[64:], 64, 1)
            ex[offset, k // few_k, k % few_k] = summed
        return carry

    lax.fori_loop(0, local_k, one_exchange, 0)
    hops = []
    distance = 1
    taken = 0
    while distance < shards:
        hop = []
        for i in range(shards // (2 * distance)):
            block = partner_of(distance) % (2 * distance) + 2 * distance * i
            if 2 * distance < shards:
                source, target = ex.at[:, block], ex_recv.at[taken]
            else:
                source, target = far_send, far_recv
            hop.append((to_partner(5, taken, distance, source, target), taken, distance, i))
            taken += 1
        hops.append(hop)
        distance *= 2
    ex_copies = [copy for hop in hops for copy, _, _, _ in hop]

    def start_hop(index):
        if index + 1 == len(hops):
            far_send[...] = ex[:, partner_of(shards // 2)].astype(jnp.bfloat16)
        for copy, _, _, _ in hops[index]:
            copy.start()

    def end_hop(index):
        for copy, slot, distance, i in hops[index]:
            copy.wait()
            if index + 1 < len(hops):
                block = me % (2 * distance) + 2 * distance * i

                def add(k, carry, slot=slot, block=block):
                    for offset in range(NOFF):
                        ex[offset, block, k] = ex[offset, block, k] + ex_recv[slot, offset, k]
                    return carry

                lax.fori_loop(0, few_k, add, 0)

    start_hop(0)

    rows[...] = jnp.zeros_like(rows)

    def write_out(offset):
        narrow = lax.broadcasted_iota(jnp.int32, (few_k, 128), 1) < 64
        for pair in range(32):
            even, odd = rows[offset, :, 2 * pair, :], rows[offset, :, 2 * pair + 1, :]
            place = pl.ds(pair * 128, 128)
            out[offset, 0, :, place] = jnp.where(narrow, even, pltpu.roll(odd, 64, 1))
            out[offset, 1, :, place] = jnp.where(narrow, pltpu.roll(even, 64, 1), odd)

    together = 2 if few_k % 2 == 0 else 1
    big = slab * shards

    for offset in range(NOFF):
        finish(len(steps))
        for copy in vv_copies[offset]:
            copy.wait_recv()
        mine[3 + 2 * offset].wait()
        load = pltpu.make_async_copy(vv_land.at[offset], vv_here, load_sem.at[0])
        load.start()
        if offset == 0:
            for copy in screen_ka:
                copy.wait_recv()
        load.wait()

        def one_image(index, carry, offset=offset):
            first = (index // shards) * together
            part = index % shards
            right = jnp.concatenate(
                [vv_here[first + i].reshape(big, 128) for i in range(together)], axis=1
            )
            left = wide[offset, part].reshape(slab, big)
            made = jnp.dot(left, right, preferred_element_type=jnp.float32)
            made = made.astype(jnp.bfloat16)
            for i in range(together):
                image[first + i, part] = made[:, i * 128 : (i + 1) * 128]
            return carry

        lax.fori_loop(0, few_k // together * shards, one_image, 0)
        if offset == 0:
            end_hop(0)
            start_hop(1)
        else:
            end_hop(len(hops) - 1)

            def add_far(k, carry):
                for each in range(NOFF):
                    total = ex[each, me, k] + far_recv[each, k].astype(jnp.float32)
                    rows[each, k] = rows[each, k] + 2.0 * total
                return carry

            lax.fori_loop(0, few_k, add_far, 0)
            write_out(0)

        def bring(source, offset=offset):
            return pltpu.make_async_copy(
                cc_land.at[offset, :, source], cc_here.at[:, source], load_sem.at[1]
            )

        def add_slab(source):
            def one_slab(k, carry):
                totals[k] = totals[k] + over_rows(image[k, source], cc_here[k, source])
                return carry

            lax.fori_loop(0, few_k, one_slab, 0)

        totals[...] = jnp.zeros_like(totals)
        mine[2 + 2 * offset].wait()
        load = bring(me)
        load.start()
        load.wait()
        add_slab(me)
        for step, copy in zip(steps, cc_copies[offset]):
            copy.wait_recv()
            source = (me + shards - step) % shards
            load = bring(source)
            load.start()
            load.wait()
            add_slab(source)
            if offset == 0:
                finish(1)

        def one_direct(k, carry, offset=offset):
            full = totals[k]
            summed = pltpu.roll(full[64:], 64, 1) + sign * full[:64]
            direct = block_transpose(summed.reshape(8, 8, 128)).reshape(64, 128)
            rows[offset, k] = rows[offset, k] - direct
            return carry

        lax.fori_loop(0, few_k, one_direct, 0)
        if offset == 0:
            for index in range(1, len(hops) - 1):
                end_hop(index)
                start_hop(index + 1)
    write_out(1)

    finish(len(steps))
    ahead.wait_send()
    for copy in screen_ga + screen_ka:
        copy.wait_send()


def local(shards, groups, pair_vc, coulomb, dens_cc, dens_vv, screen, offsets):
    local_k, slab, width = pair_vc.shape
    few_k = local_k // shards
    big = slab * shards
    spread = jnp.broadcast_to(coulomb[:, None], (slab, width))
    land = jax.ShapeDtypeStruct((NOFF, few_k, shards, slab, width), jnp.bfloat16)
    anywhere = pl.BlockSpec(memory_space=pl.ANY)
    in_vmem = pl.BlockSpec(memory_space=pltpu.VMEM)
    flops = 2 * NOFF * (few_k * big * big * width + 2 * few_k * big * width * width)
    result = pl.pallas_call(
        functools.partial(kernel, shards, groups),
        out_shape=[
            jax.ShapeDtypeStruct((NOFF, 2, few_k, 4096), jnp.float32),
            land,
            land,
        ],
        in_specs=[pl.BlockSpec(memory_space=pltpu.SMEM), in_vmem] + [anywhere] * 4,
        out_specs=[in_vmem, anywhere, anywhere],
        scratch_shapes=[
            pltpu.VMEM((2 * local_k, slab, width), jnp.bfloat16),
            pltpu.VMEM((NOFF, shards, few_k, 64, 128), jnp.float32),
            pltpu.VMEM((shards - 2, NOFF, few_k, 64, 128), jnp.float32),
            pltpu.VMEM((NOFF, few_k, 64, 128), jnp.bfloat16),
            pltpu.VMEM((NOFF, few_k, 64, 128), jnp.bfloat16),
            pltpu.VMEM((NOFF, shards, groups, slab // groups, big), jnp.bfloat16),
            pltpu.VMEM((few_k, shards, slab, width), jnp.bfloat16),
            pltpu.VMEM((few_k, shards, slab, width), jnp.bfloat16),
            pltpu.VMEM((few_k, shards, slab, width), jnp.bfloat16),
            pltpu.VMEM((few_k, 128, 128), jnp.float32),
            pltpu.VMEM((NOFF, few_k, 64, 128), jnp.float32),
            pltpu.SemaphoreType.DMA((6, shards)),
            pltpu.SemaphoreType.DMA((6, shards)),
            pltpu.SemaphoreType.DMA((groups,)),
            pltpu.SemaphoreType.DMA((groups,)),
            pltpu.SemaphoreType.DMA((6,)),
            pltpu.SemaphoreType.DMA((2,)),
        ],
        compiler_params=pltpu.CompilerParams(
            collective_id=0, has_side_effects=True, vmem_limit_bytes=62 * 1024 * 1024
        ),
        cost_estimate=pl.CostEstimate(flops=flops, bytes_accessed=80_000_000, transcendentals=0),
        name="bse_blocks",
    )(offsets, spread, pair_vc, dens_cc, dens_vv, screen)
    return result[0]


def solution(mesh):
    placed = (
        P("ka", "ga", None),
        P("ga"),
        P(None, "ka", "ga", None),
        P(None, "ka", "ga", None),
        P(None, "ga", None),
        P(),
    )
    return jax.shard_map(
        functools.partial(local, mesh.shape["ga"], mesh.shape["ka"]),
        mesh=mesh,
        in_specs=placed,
        out_specs=P(None, None, ("ka", "ga"), None),
        check_vma=False,
    )
```

```python
import functools

import jax
import jax.numpy as jnp
from jax import lax
from jax.experimental import pallas as pl
from jax.experimental.pallas import tpu as pltpu
from jax.sharding import PartitionSpec as P

NV = 8
NC = 8
NKY = 24
NOFF = 2
WINDOW = 6
MESH = pl.DeviceIdType.MESH


def step_order(length):
    half = length // 2
    order = [half]
    for near in range(1, half):
        order += [near, half + near]
    return order


def over_rows(left, right):
    return lax.dot_general(
        left, right, (((0,), (0,)), ((), ())), preferred_element_type=jnp.float32
    )


def block_transpose(tile):
    row = lax.broadcasted_iota(jnp.int32, tile.shape, 1)
    lane = lax.broadcasted_iota(jnp.int32, tile.shape, 2)
    for bit in range(3):
        size = 1 << bit
        row_bit = (row // size) % 2
        lane_bit = (lane // (8 * size)) % 2
        down = pltpu.roll(pltpu.roll(tile, 8 - size, 1), 8 * size, 2)
        up = pltpu.roll(pltpu.roll(tile, size, 1), 128 - 8 * size, 2)
        tile = jnp.where(row_bit == lane_bit, tile, jnp.where(row_bit == 0, down, up))
    return tile


def kernel(
    shards, groups, offsets, coulomb, pair_vc, dens_cc, dens_vv, screen,
    out, cc_land, vv_land,
    both, ex, ex_recv, far_send, far_recv, wide, vv_here, cc_here, image, totals, rows,
    send_sem, recv_sem, ka_send, ka_recv, own_sem, load_sem,
):
    me = lax.axis_index("ga")
    my_ka = lax.axis_index("ka")
    local_k, slab, _ = pair_vc.shape
    few_k = local_k // shards
    quarter = slab // groups
    steps = step_order(shards)
    lane = lax.broadcasted_iota(jnp.int32, (64, 128), 1)
    sign = jnp.where(lane < 64, 1.0, -1.0)

    barrier = pltpu.get_barrier_semaphore()
    for step in range(1, shards):
        pl.semaphore_signal(
            barrier, inc=1, device_id={"ga": (me + step) % shards}, device_id_type=MESH
        )
    for step in range(1, groups):
        pl.semaphore_signal(
            barrier, inc=1, device_id={"ka": (my_ka + step) % groups}, device_id_type=MESH
        )
    pl.semaphore_wait(barrier, shards - 1 + groups - 1)

    def own(index, source, target):
        return pltpu.make_async_copy(source, target, own_sem.at[index])

    def flipped(index, distance, length):
        bit = 1
        while bit < length:
            if distance & bit:
                index = index + bit - 2 * bit * ((index // bit) % 2)
            bit *= 2
        return index

    def partner_of(distance):
        return flipped(me, distance, shards)

    def to_partner(kind, index, distance, source, target):
        return pltpu.make_async_remote_copy(
            src_ref=source,
            dst_ref=target,
            send_sem=send_sem.at[kind, index],
            recv_sem=recv_sem.at[kind, index],
            device_id={"ga": partner_of(distance)},
            device_id_type=MESH,
        )

    def to_ka(index, peer, source, target):
        return pltpu.make_async_remote_copy(
            src_ref=source,
            dst_ref=target,
            send_sem=ka_send.at[index],
            recv_sem=ka_recv.at[index],
            device_id={"ka": peer},
            device_id_type=MESH,
        )

    def dens_copies(kind, dens, land, offset):
        return [
            to_partner(
                kind,
                step,
                step,
                dens.at[offset, pl.ds(partner_of(step) * few_k, few_k)],
                land.at[offset, :, me],
            )
            for step in steps
        ]

    ahead = to_ka(0, (my_ka + groups - 1) % groups, pair_vc, both.at[pl.ds(local_k, local_k)])
    ahead.start()
    my_rows = screen.at[:, pl.ds(my_ka * quarter, quarter)]
    screen_hops = []
    distance = shards // 2
    taken = 0
    while distance >= 1:
        hop = []
        for i in range(shards // (2 * distance)):
            block = me % (2 * distance) + 2 * distance * i
            place = wide.at[:, block, my_ka]
            hop.append(to_partner(4, taken, distance, my_rows if taken == 0 else place, place))
            taken += 1
        screen_hops.append(hop)
        distance //= 2
    screen_ga = sum(screen_hops, [])
    for copy in screen_hops[0]:
        copy.start()
    mine = [
        own(0, pair_vc, both.at[pl.ds(0, local_k)]),
        own(1, my_rows, wide.at[:, me, my_ka]),
    ]
    for offset in range(NOFF):
        for index, dens, land in ((2, dens_cc, cc_land), (3, dens_vv, vv_land)):
            mine.append(
                own(
                    index + 2 * offset,
                    dens.at[offset, pl.ds(me * few_k, few_k)],
                    land.at[offset, :, me],
                )
            )
    for copy in mine:
        copy.start()

    vv_copies = [dens_copies(offset, dens_vv, vv_land, offset) for offset in range(NOFF)]
    cc_copies = [dens_copies(2 + offset, dens_cc, cc_land, offset) for offset in range(NOFF)]
    queue = []
    for offset in range(NOFF):
        queue += vv_copies[offset] + cc_copies[offset]
    sent = [0, 0]

    def finish(count):
        for _ in range(count):
            queue[sent[1]].wait_send()
            sent[1] += 1
            if sent[0] < len(queue):
                queue[sent[0]].start()
                sent[0] += 1

    while sent[0] < min(WINDOW, len(queue)):
        queue[sent[0]].start()
        sent[0] += 1

    mine[1].wait()
    for index, hop in enumerate(screen_hops):
        for copy in hop:
            copy.wait_recv()
        if index + 1 < len(screen_hops):
            for copy in screen_hops[index + 1]:
                copy.start()
    screen_ka_hops = []
    distance = groups // 2
    taken = 1
    while distance >= 1:
        hop = []
        for i in range(groups // (2 * distance)):
            part = wide.at[:, :, my_ka % (2 * distance) + 2 * distance * i]
            hop.append(to_ka(taken, flipped(my_ka, distance, groups), part, part))
            taken += 1
        screen_ka_hops.append(hop)
        distance //= 2
    screen_ka = sum(screen_ka_hops, [])
    for copy in screen_ka_hops[0]:
        copy.start()
    finish(2)

    mine[0].wait()
    ahead.wait_recv()

    def one_exchange(k, carry):
        scaled = (coulomb[...] * both[k].astype(jnp.float32)).astype(jnp.bfloat16)
        row, column = k // NKY, k % NKY
        for offset in range(NOFF):
            moved_column = column + offsets[offset, 1]
            moved_column = jnp.where(moved_column >= NKY, moved_column - NKY, moved_column)
            partner = (row + offsets[offset, 0]) * NKY + moved_column
            full = over_rows(scaled, both[partner])
            summed = full[:64] + sign * pltpu.roll(full[64:], 64, 1)
            ex[offset, k // few_k, k % few_k] = summed
        return carry

    lax.fori_loop(0, local_k // 2, one_exchange, 0)
    finish(1)
    lax.fori_loop(local_k // 2, local_k, one_exchange, 0)
    for index in range(1, len(screen_ka_hops)):
        for copy in screen_ka_hops[index - 1]:
            copy.wait_recv()
        for copy in screen_ka_hops[index]:
            copy.start()
    hops = []
    distance = 1
    taken = 0
    while distance < shards:
        hop = []
        for i in range(shards // (2 * distance)):
            block = partner_of(distance) % (2 * distance) + 2 * distance * i
            if 2 * distance < shards:
                source, target = ex.at[:, block], ex_recv.at[taken]
            else:
                source, target = far_send, far_recv
            hop.append((to_partner(5, taken, distance, source, target), taken, distance, i))
            taken += 1
        hops.append(hop)
        distance *= 2
    ex_copies = [copy for hop in hops for copy, _, _, _ in hop]

    def start_hop(index):
        if index + 1 == len(hops):
            far_send[...] = ex[:, partner_of(shards // 2)].astype(jnp.bfloat16)
        for copy, _, _, _ in hops[index]:
            copy.start()

    def end_hop(index):
        for copy, slot, distance, i in hops[index]:
            copy.wait()
            if index + 1 < len(hops):
                block = me % (2 * distance) + 2 * distance * i

                def add(k, carry, slot=slot, block=block):
                    for offset in range(NOFF):
                        ex[offset, block, k] = ex[offset, block, k] + ex_recv[slot, offset, k]
                    return carry

                lax.fori_loop(0, few_k, add, 0)

    start_hop(0)

    rows[...] = jnp.zeros_like(rows)

    def write_out(offset):
        narrow = lax.broadcasted_iota(jnp.int32, (few_k, 128), 1) < 64
        for pair in range(32):
            even, odd = rows[offset, :, 2 * pair, :], rows[offset, :, 2 * pair + 1, :]
            place = pl.ds(pair * 128, 128)
            out[offset, 0, :, place] = jnp.where(narrow, even, pltpu.roll(odd, 64, 1))
            out[offset, 1, :, place] = jnp.where(narrow, pltpu.roll(even, 64, 1), odd)

    together = 2 if few_k % 2 == 0 else 1
    big = slab * shards

    for offset in range(NOFF):
        finish(len(steps) - 3 if offset == 0 else len(steps))
        for copy in vv_copies[offset]:
            copy.wait_recv()
        mine[3 + 2 * offset].wait()
        load = pltpu.make_async_copy(vv_land.at[offset], vv_here, load_sem.at[0])
        load.start()
        if offset == 0:
            for copy in screen_ka_hops[-1]:
                copy.wait_recv()
        load.wait()

        def one_image(index, carry, offset=offset):
            first = (index // shards) * together
            part = index % shards
            right = jnp.concatenate(
                [vv_here[first + i].reshape(big, 128) for i in range(together)], axis=1
            )
            left = wide[offset, part].reshape(slab, big)
            made = jnp.dot(left, right, preferred_element_type=jnp.float32)
            made = made.astype(jnp.bfloat16)
            for i in range(together):
                image[first + i, part] = made[:, i * 128 : (i + 1) * 128]
            return carry

        lax.fori_loop(0, few_k // together * shards, one_image, 0)
        if offset == 0:
            end_hop(0)
            start_hop(1)
        else:
            end_hop(len(hops) - 1)

            def add_far(k, carry):
                for each in range(NOFF):
                    total = ex[each, me, k] + far_recv[each, k].astype(jnp.float32)
                    rows[each, k] = rows[each, k] + 2.0 * total
                return carry

            lax.fori_loop(0, few_k, add_far, 0)
            write_out(0)

        def bring(source, offset=offset):
            return pltpu.make_async_copy(
                cc_land.at[offset, :, source], cc_here.at[:, source], load_sem.at[1]
            )

        def add_slab(source):
            def one_slab(k, carry):
                totals[k] = totals[k] + over_rows(image[k, source], cc_here[k, source])
                return carry

            lax.fori_loop(0, few_k, one_slab, 0)

        totals[...] = jnp.zeros_like(totals)
        mine[2 + 2 * offset].wait()
        load = bring(me)
        load.start()
        load.wait()
        add_slab(me)
        for step, copy in zip(steps, cc_copies[offset]):
            finish(1)
            copy.wait_recv()
            source = partner_of(step)
            load = bring(source)
            load.start()
            load.wait()
            add_slab(source)

        def one_direct(k, carry, offset=offset):
            full = totals[k]
            summed = pltpu.roll(full[64:], 64, 1) + sign * full[:64]
            direct = block_transpose(summed.reshape(8, 8, 128)).reshape(64, 128)
            rows[offset, k] = rows[offset, k] - direct
            return carry

        lax.fori_loop(0, few_k, one_direct, 0)
        if offset == 0:
            for index in range(1, len(hops) - 1):
                end_hop(index)
                start_hop(index + 1)
    write_out(1)

    ahead.wait_send()
    for copy in screen_ga + screen_ka:
        copy.wait_send()


def local(shards, groups, pair_vc, coulomb, dens_cc, dens_vv, screen, offsets):
    local_k, slab, width = pair_vc.shape
    few_k = local_k // shards
    big = slab * shards
    spread = jnp.broadcast_to(coulomb[:, None], (slab, width))
    land = jax.ShapeDtypeStruct((NOFF, few_k, shards, slab, width), jnp.bfloat16)
    anywhere = pl.BlockSpec(memory_space=pl.ANY)
    in_vmem = pl.BlockSpec(memory_space=pltpu.VMEM)
    flops = 2 * NOFF * (few_k * big * big * width + 2 * few_k * big * width * width)
    result = pl.pallas_call(
        functools.partial(kernel, shards, groups),
        out_shape=[
            jax.ShapeDtypeStruct((NOFF, 2, few_k, 4096), jnp.float32),
            land,
            land,
        ],
        in_specs=[pl.BlockSpec(memory_space=pltpu.SMEM), in_vmem] + [anywhere] * 4,
        out_specs=[in_vmem, anywhere, anywhere],
        scratch_shapes=[
            pltpu.VMEM((2 * local_k, slab, width), jnp.bfloat16),
            pltpu.VMEM((NOFF, shards, few_k, 64, 128), jnp.float32),
            pltpu.VMEM((shards - 2, NOFF, few_k, 64, 128), jnp.float32),
            pltpu.VMEM((NOFF, few_k, 64, 128), jnp.bfloat16),
            pltpu.VMEM((NOFF, few_k, 64, 128), jnp.bfloat16),
            pltpu.VMEM((NOFF, shards, groups, slab // groups, big), jnp.bfloat16),
            pltpu.VMEM((few_k, shards, slab, width), jnp.bfloat16),
            pltpu.VMEM((few_k, shards, slab, width), jnp.bfloat16),
            pltpu.VMEM((few_k, shards, slab, width), jnp.bfloat16),
            pltpu.VMEM((few_k, 128, 128), jnp.float32),
            pltpu.VMEM((NOFF, few_k, 64, 128), jnp.float32),
            pltpu.SemaphoreType.DMA((6, shards)),
            pltpu.SemaphoreType.DMA((6, shards)),
            pltpu.SemaphoreType.DMA((groups,)),
            pltpu.SemaphoreType.DMA((groups,)),
            pltpu.SemaphoreType.DMA((6,)),
            pltpu.SemaphoreType.DMA((2,)),
        ],
        compiler_params=pltpu.CompilerParams(
            collective_id=0, has_side_effects=True, vmem_limit_bytes=62 * 1024 * 1024
        ),
        cost_estimate=pl.CostEstimate(flops=flops, bytes_accessed=80_000_000, transcendentals=0),
        name="bse_blocks",
    )(offsets, spread, pair_vc, dens_cc, dens_vv, screen)
    return result[0]


def solution(mesh):
    placed = (
        P("ka", "ga", None),
        P("ga"),
        P(None, "ka", "ga", None),
        P(None, "ka", "ga", None),
        P(None, "ga", None),
        P(),
    )
    return jax.shard_map(
        functools.partial(local, mesh.shape["ga"], mesh.shape["ka"]),
        mesh=mesh,
        in_specs=placed,
        out_specs=P(None, None, ("ka", "ga"), None),
        check_vma=False,
    )
```

```python
import functools

import jax
import jax.numpy as jnp
from jax import lax
from jax.experimental import pallas as pl
from jax.experimental.pallas import tpu as pltpu
from jax.sharding import PartitionSpec as P

NV = 8
NC = 8
NKY = 24
NOFF = 2
WINDOW = 10
MESH = pl.DeviceIdType.MESH


def step_order(length):
    order = []
    for i in range(length):
        step = length // 2 + (i + 1) // 2 * (1 if i % 2 else -1)
        if 0 < step < length:
            order.append(step)
    return order


def over_rows(left, right):
    return lax.dot_general(
        left, right, (((0,), (0,)), ((), ())), preferred_element_type=jnp.float32
    )


def block_transpose(tile):
    row = lax.broadcasted_iota(jnp.int32, tile.shape, 1)
    lane = lax.broadcasted_iota(jnp.int32, tile.shape, 2)
    for bit in range(3):
        size = 1 << bit
        row_bit = (row // size) % 2
        lane_bit = (lane // (8 * size)) % 2
        down = pltpu.roll(pltpu.roll(tile, 8 - size, 1), 8 * size, 2)
        up = pltpu.roll(pltpu.roll(tile, size, 1), 128 - 8 * size, 2)
        tile = jnp.where(row_bit == lane_bit, tile, jnp.where(row_bit == 0, down, up))
    return tile


def kernel(
    shards, groups, offsets, coulomb, pair_vc, dens_cc, dens_vv, screen,
    out, cc_land, vv_land,
    both, ex, ex_recv, far_send, far_recv, wide, vv_here, cc_here, image, rows,
    send_sem, recv_sem, ka_send, ka_recv, own_sem, load_sem,
):
    me = lax.axis_index("ga")
    my_ka = lax.axis_index("ka")
    local_k, slab, _ = pair_vc.shape
    few_k = local_k // shards
    quarter = slab // groups
    steps = step_order(shards)
    lane = lax.broadcasted_iota(jnp.int32, (64, 128), 1)
    sign = jnp.where(lane < 64, 1.0, -1.0)

    barrier = pltpu.get_barrier_semaphore()
    for step in range(1, shards):
        pl.semaphore_signal(
            barrier, inc=1, device_id={"ga": (me + step) % shards}, device_id_type=MESH
        )
    for step in range(1, groups):
        pl.semaphore_signal(
            barrier, inc=1, device_id={"ka": (my_ka + step) % groups}, device_id_type=MESH
        )
    pl.semaphore_wait(barrier, shards - 1 + groups - 1)

    def own(index, source, target):
        return pltpu.make_async_copy(source, target, own_sem.at[index])

    def to_ga(kind, step, source, target):
        return pltpu.make_async_remote_copy(
            src_ref=source,
            dst_ref=target,
            send_sem=send_sem.at[kind, step],
            recv_sem=recv_sem.at[kind, step],
            device_id={"ga": (me + step) % shards},
            device_id_type=MESH,
        )

    def partner_of(distance):
        return me + distance - 2 * distance * ((me // distance) % 2)

    def to_partner(kind, index, distance, source, target):
        return pltpu.make_async_remote_copy(
            src_ref=source,
            dst_ref=target,
            send_sem=send_sem.at[kind, index],
            recv_sem=recv_sem.at[kind, index],
            device_id={"ga": partner_of(distance)},
            device_id_type=MESH,
        )

    def to_ka(index, peer, source, target):
        return pltpu.make_async_remote_copy(
            src_ref=source,
            dst_ref=target,
            send_sem=ka_send.at[index],
            recv_sem=ka_recv.at[index],
            device_id={"ka": peer},
            device_id_type=MESH,
        )

    def dens_copies(kind, dens, land, offset):
        return [
            to_ga(
                kind,
                step,
                dens.at[offset, pl.ds(((me + step) % shards) * few_k, few_k)],
                land.at[offset, :, me],
            )
            for step in steps
        ]

    ahead = to_ka(0, (my_ka + groups - 1) % groups, pair_vc, both.at[pl.ds(local_k, local_k)])
    ahead.start()
    my_rows = screen.at[:, pl.ds(my_ka * quarter, quarter)]
    screen_hops = []
    distance = shards // 2
    taken = 0
    while distance >= 1:
        hop = []
        for i in range(shards // (2 * distance)):
            block = me % (2 * distance) + 2 * distance * i
            place = wide.at[:, block, my_ka]
            hop.append(to_partner(4, taken, distance, my_rows if taken == 0 else place, place))
            taken += 1
        screen_hops.append(hop)
        distance //= 2
    screen_ga = sum(screen_hops, [])
    for copy in screen_hops[0]:
        copy.start()
    mine = [
        own(0, pair_vc, both.at[pl.ds(0, local_k)]),
        own(1, my_rows, wide.at[:, me, my_ka]),
    ]
    for offset in range(NOFF):
        for index, dens, land in ((2, dens_cc, cc_land), (3, dens_vv, vv_land)):
            mine.append(
                own(
                    index + 2 * offset,
                    dens.at[offset, pl.ds(me * few_k, few_k)],
                    land.at[offset, :, me],
                )
            )
    for copy in mine:
        copy.start()

    vv_copies = [dens_copies(offset, dens_vv, vv_land, offset) for offset in range(NOFF)]
    cc_copies = [dens_copies(2 + offset, dens_cc, cc_land, offset) for offset in range(NOFF)]
    queue = []
    for offset in range(NOFF):
        queue += vv_copies[offset] + cc_copies[offset]
    sent = [0, 0]

    def finish(count):
        for _ in range(count):
            queue[sent[1]].wait_send()
            sent[1] += 1
            if sent[0] < len(queue):
                queue[sent[0]].start()
                sent[0] += 1

    while sent[0] < min(WINDOW, len(queue)):
        queue[sent[0]].start()
        sent[0] += 1

    mine[1].wait()
    for index, hop in enumerate(screen_hops):
        for copy in hop:
            copy.wait_recv()
        if index + 1 < len(screen_hops):
            for copy in screen_hops[index + 1]:
                copy.start()
    screen_ka_hops = []
    distance = groups // 2
    taken = 1
    while distance >= 1:
        hop = []
        for i in range(groups // (2 * distance)):
            part = wide.at[:, :, my_ka % (2 * distance) + 2 * distance * i]
            peer = my_ka + distance - 2 * distance * ((my_ka // distance) % 2)
            hop.append(to_ka(taken, peer, part, part))
            taken += 1
        screen_ka_hops.append(hop)
        distance //= 2
    screen_ka = sum(screen_ka_hops, [])
    for copy in screen_ka_hops[0]:
        copy.start()

    mine[0].wait()
    ahead.wait_recv()

    def one_exchange(k, carry):
        scaled = (coulomb[...] * both[k].astype(jnp.float32)).astype(jnp.bfloat16)
        row, column = k // NKY, k % NKY
        for offset in range(NOFF):
            moved_column = column + offsets[offset, 1]
            moved_column = jnp.where(moved_column >= NKY, moved_column - NKY, moved_column)
            partner = (row + offsets[offset, 0]) * NKY + moved_column
            full = over_rows(scaled, both[partner])
            summed = full[:64] + sign * pltpu.roll(full[64:], 64, 1)
            ex[offset, k // few_k, k % few_k] = summed
        return carry

    lax.fori_loop(0, local_k, one_exchange, 0)
    for index in range(1, len(screen_ka_hops)):
        for copy in screen_ka_hops[index - 1]:
            copy.wait_recv()
        for copy in screen_ka_hops[index]:
            copy.start()
    hops = []
    distance = 1
    taken = 0
    while distance < shards:
        hop = []
        for i in range(shards // (2 * distance)):
            block = partner_of(distance) % (2 * distance) + 2 * distance * i
            if 2 * distance < shards:
                source, target = ex.at[:, block], ex_recv.at[taken]
            else:
                source, target = far_send, far_recv
            hop.append((to_partner(5, taken, distance, source, target), taken, distance, i))
            taken += 1
        hops.append(hop)
        distance *= 2
    ex_copies = [copy for hop in hops for copy, _, _, _ in hop]

    def start_hop(index):
        if index + 1 == len(hops):
            far_send[...] = ex[:, partner_of(shards // 2)].astype(jnp.bfloat16)
        for copy, _, _, _ in hops[index]:
            copy.start()

    def end_hop(index):
        for copy, slot, distance, i in hops[index]:
            copy.wait()
            if index + 1 < len(hops):
                block = me % (2 * distance) + 2 * distance * i

                def add(k, carry, slot=slot, block=block):
                    for offset in range(NOFF):
                        ex[offset, block, k] = ex[offset, block, k] + ex_recv[slot, offset, k]
                    return carry

                lax.fori_loop(0, few_k, add, 0)

    start_hop(0)

    rows[...] = jnp.zeros_like(rows)

    def write_out(offset):
        narrow = lax.broadcasted_iota(jnp.int32, (few_k, 128), 1) < 64
        for pair in range(32):
            even, odd = rows[offset, :, 2 * pair, :], rows[offset, :, 2 * pair + 1, :]
            place = pl.ds(pair * 128, 128)
            out[offset, 0, :, place] = jnp.where(narrow, even, pltpu.roll(odd, 64, 1))
            out[offset, 1, :, place] = jnp.where(narrow, pltpu.roll(even, 64, 1), odd)

    together = 2 if few_k % 2 == 0 else 1
    big = slab * shards

    for offset in range(NOFF):
        finish(len(steps))
        for copy in vv_copies[offset]:
            copy.wait_recv()
        mine[3 + 2 * offset].wait()
        load = pltpu.make_async_copy(vv_land.at[offset], vv_here, load_sem.at[0])
        load.start()
        if offset == 0:
            for copy in screen_ka_hops[-1]:
                copy.wait_recv()
        load.wait()

        def one_image(index, carry, offset=offset):
            first = (index // shards) * together
            part = index % shards
            right = jnp.concatenate(
                [vv_here[first + i].reshape(big, 128) for i in range(together)], axis=1
            )
            left = wide[offset, part].reshape(slab, big)
            made = jnp.dot(left, right, preferred_element_type=jnp.float32)
            made = made.astype(jnp.bfloat16)
            for i in range(together):
                image[first + i, part] = made[:, i * 128 : (i + 1) * 128]
            return carry

        lax.fori_loop(0, few_k // together * shards, one_image, 0)
        if offset == 0:
            end_hop(0)
            start_hop(1)
        else:
            end_hop(len(hops) - 1)

            def add_far(k, carry):
                for each in range(NOFF):
                    total = ex[each, me, k] + far_recv[each, k].astype(jnp.float32)
                    rows[each, k] = rows[each, k] + 2.0 * total
                return carry

            lax.fori_loop(0, few_k, add_far, 0)
            write_out(0)

        finish(len(steps))
        for copy in cc_copies[offset]:
            copy.wait_recv()
        mine[2 + 2 * offset].wait()
        load = pltpu.make_async_copy(cc_land.at[offset], cc_here, load_sem.at[1])
        load.start()
        load.wait()

        def one_direct(k, carry, offset=offset):
            full = over_rows(image[k].reshape(big, 128), cc_here[k].reshape(big, 128))
            summed = pltpu.roll(full[64:], 64, 1) + sign * full[:64]
            direct = block_transpose(summed.reshape(8, 8, 128)).reshape(64, 128)
            rows[offset, k] = rows[offset, k] - direct
            return carry

        lax.fori_loop(0, few_k, one_direct, 0)
        if offset == 0:
            for index in range(1, len(hops) - 1):
                end_hop(index)
                start_hop(index + 1)
    write_out(1)

    ahead.wait_send()
    for copy in screen_ga + screen_ka:
        copy.wait_send()


def local(shards, groups, pair_vc, coulomb, dens_cc, dens_vv, screen, offsets):
    local_k, slab, width = pair_vc.shape
    few_k = local_k // shards
    big = slab * shards
    spread = jnp.broadcast_to(coulomb[:, None], (slab, width))
    land = jax.ShapeDtypeStruct((NOFF, few_k, shards, slab, width), jnp.bfloat16)
    anywhere = pl.BlockSpec(memory_space=pl.ANY)
    in_vmem = pl.BlockSpec(memory_space=pltpu.VMEM)
    flops = 2 * NOFF * (few_k * big * big * width + 2 * few_k * big * width * width)
    result = pl.pallas_call(
        functools.partial(kernel, shards, groups),
        out_shape=[
            jax.ShapeDtypeStruct((NOFF, 2, few_k, 4096), jnp.float32),
            land,
            land,
        ],
        in_specs=[pl.BlockSpec(memory_space=pltpu.SMEM), in_vmem] + [anywhere] * 4,
        out_specs=[in_vmem, anywhere, anywhere],
        scratch_shapes=[
            pltpu.VMEM((2 * local_k, slab, width), jnp.bfloat16),
            pltpu.VMEM((NOFF, shards, few_k, 64, 128), jnp.float32),
            pltpu.VMEM((shards - 2, NOFF, few_k, 64, 128), jnp.float32),
            pltpu.VMEM((NOFF, few_k, 64, 128), jnp.bfloat16),
            pltpu.VMEM((NOFF, few_k, 64, 128), jnp.bfloat16),
            pltpu.VMEM((NOFF, shards, groups, slab // groups, big), jnp.bfloat16),
            pltpu.VMEM((few_k, shards, slab, width), jnp.bfloat16),
            pltpu.VMEM((few_k, shards, slab, width), jnp.bfloat16),
            pltpu.VMEM((few_k, shards, slab, width), jnp.bfloat16),
            pltpu.VMEM((NOFF, few_k, 64, 128), jnp.float32),
            pltpu.SemaphoreType.DMA((6, shards)),
            pltpu.SemaphoreType.DMA((6, shards)),
            pltpu.SemaphoreType.DMA((groups,)),
            pltpu.SemaphoreType.DMA((groups,)),
            pltpu.SemaphoreType.DMA((6,)),
            pltpu.SemaphoreType.DMA((2,)),
        ],
        compiler_params=pltpu.CompilerParams(
            collective_id=0, has_side_effects=True, vmem_limit_bytes=62 * 1024 * 1024
        ),
        cost_estimate=pl.CostEstimate(flops=flops, bytes_accessed=80_000_000, transcendentals=0),
        name="bse_blocks",
    )(offsets, spread, pair_vc, dens_cc, dens_vv, screen)
    return result[0]


def solution(mesh):
    placed = (
        P("ka", "ga", None),
        P("ga"),
        P(None, "ka", "ga", None),
        P(None, "ka", "ga", None),
        P(None, "ga", None),
        P(),
    )
    return jax.shard_map(
        functools.partial(local, mesh.shape["ga"], mesh.shape["ka"]),
        mesh=mesh,
        in_specs=placed,
        out_specs=P(None, None, ("ka", "ga"), None),
        check_vma=False,
    )
```
